32 devices in a mesh: cells: 32 (over z, y, x, core).
Axes of the slice: x: 2, y: 2, z: 4, core: 2. Of those that a mesh axis runs over, the one named last changes fastest.
Arguments:
- source_points: bfloat16 [50, 32768], P(None, 'cells'), may hold values from -15 to 15
- target_points: bfloat16 [50, 32768], P(None, 'cells'), may hold values from -15 to 15
- target_features: bfloat16 [32768, 256], P('cells'), may hold values from -6 to 6
- source_mass: float32 [32768], P('cells'), may hold values from -1 to 1
- target_mass: float32 [32768], P('cells'), may hold values from -1 to 1
- pair_list: int32 [3, 384], P(None, 'cells'), may hold values from 0 to 31, as said below
Outputs:
- source_potential: float32 [32768], P('cells')
- target_potential: float32 [32768], P('cells')
- mapped_features: bfloat16 [32768, 256], P('cells')
The draws below stay inside these ranges and needn't reach their ends.
Inputs may be any that keep to these rules, and one draw needn't show every extreme that they name: `pair_list`: column s is a slot of device s // 12: row 0 names a source block, row 1 a target block, row 2 is 1 where the slot holds a pair and 0 where it is empty; a device's live slots come first, in an order drawn from the seed, and an empty slot names the device's own block twice. Each source block is paired with 7 target blocks within 4 blocks of it around the cycle of 32 blocks: its own, and others drawn from the seed; every pair is listed once. A pair's owner lies in the aligned group of 4 devices that holds its source block; in every group one device owns 12 pairs and the others share the rest as evenly as possible, in an order drawn from the seed.
All inputs are finite; a program needn't handle non-finite values.
Results may differ from the reference program's by a relative error of at most 0.01.
Values may be sent and summed in bfloat16 or wider, within the bound.
A program may use at most 128 MiB of HBM per device.

```python
import jax
import jax.numpy as jnp
from jax import lax

DIMS = 50
FEAT = 256
BLK = 1024
REACH = 4
NEIGH = 7
GROUP = 4
MOST = 12
ITERS = 2
BLOCKS = 32
CELLS = 32768
N_CELLS = 32


def draw_pair_list(key, part):
    key = jax.random.fold_in(key, 11)
    first, second, third = jax.random.split(key, 3)
    candidates = jnp.concatenate([jnp.arange(-REACH, 0), jnp.arange(1, REACH + 1)]).astype(jnp.int32)
    picks = jax.vmap(lambda entry: jax.random.permutation(entry, 2 * REACH))(jax.random.split(first, BLOCKS))
    offsets = jnp.concatenate([jnp.zeros((BLOCKS, 1), jnp.int32), candidates[picks[:, :NEIGH - 1]]], axis=1)
    orders = jax.vmap(lambda entry: jax.random.permutation(entry, NEIGH))(jax.random.split(second, BLOCKS))
    offsets = jnp.take_along_axis(offsets, orders, axis=1)
    source = jnp.repeat(jnp.arange(BLOCKS, dtype=jnp.int32), NEIGH)
    target = ((source + offsets.reshape(-1)) % BLOCKS).astype(jnp.int32)
    groups = BLOCKS // GROUP
    remainder = GROUP * NEIGH - MOST
    base_count = remainder // (GROUP - 1)
    extra_count = remainder % (GROUP - 1)
    pattern = jnp.array([MOST] + [base_count + 1] * extra_count + [base_count] * (GROUP - 1 - extra_count), jnp.int32)
    counts = jax.vmap(lambda entry: pattern[jax.random.permutation(entry, GROUP)])(jax.random.split(third, groups))
    ends = jnp.cumsum(counts, axis=1)
    starts = ends - counts
    within = jnp.arange(GROUP * NEIGH, dtype=jnp.int32)
    local_owner = jnp.sum((within[None, :, None] >= ends[:, None, :]).astype(jnp.int32), axis=2)
    slot_index = within[None, :] - jnp.take_along_axis(starts, local_owner, axis=1)
    owner = local_owner + jnp.arange(groups, dtype=jnp.int32)[:, None] * GROUP
    place = (owner * MOST + slot_index).reshape(-1).astype(jnp.int32)
    devices = (jnp.arange(BLOCKS * MOST, dtype=jnp.int32) // MOST).astype(jnp.int32)
    rows = jnp.stack([devices, devices, jnp.zeros_like(devices)]).astype(jnp.int32)
    rows = rows.at[0, place].set(source).at[1, place].set(target).at[2, place].set(1)
    return rows


def draw_source_points(key, part):
    key = jax.random.fold_in(key, 21)
    first = jax.random.fold_in(key, 0)
    values = jnp.clip(jax.random.normal(first, (DIMS, CELLS), jnp.float32), -6.0, 6.0)
    return values.astype(jnp.bfloat16)


def draw_target_points(key, part):
    key = jax.random.fold_in(key, 22)
    first = jax.random.fold_in(key, 0)
    values = jnp.clip(jax.random.normal(first, (DIMS, CELLS), jnp.float32), -6.0, 6.0)
    return values.astype(jnp.bfloat16)


def steps_of(rng, dims, shards, low, largest):
    loudness = 1.0
    for axis_at, shards_of in shards:
        heights = jax.random.uniform(jax.random.fold_in(jax.random.fold_in(rng, 6), axis_at), (shards_of,), jnp.float32, low / len(shards), largest / len(shards))
        loudness = loudness * jnp.repeat(jnp.exp(heights), dims[axis_at] // shards_of).reshape((-1,) + (1,) * (len(dims) - 1 - axis_at))
    return loudness


def centred(rng, extent, width, limit, cuts=(), kind=jnp.bfloat16):
    values = jax.random.normal(rng, extent, jnp.float32) * width
    if len(cuts) > 0:
        values = steps_of(rng, extent, cuts, -0.22, 0.18) * values
    return jnp.clip(values, min=-limit, max=limit).astype(kind)


def setup_inputs(seed: int = 0) -> dict:
    arg_keys = jax.random.split(jax.random.key(seed), 7)
    source_points = draw_source_points(jax.random.fold_in(arg_keys[6], 71), 0)
    target_points = draw_target_points(jax.random.fold_in(arg_keys[6], 71), 0)
    target_features = centred(arg_keys[2], (CELLS, FEAT), 1.0, 6.0, ((0, 32),))
    source_mass = jnp.clip(jax.random.uniform(arg_keys[3], (CELLS,), jnp.float32, -1.0, 1.0) * steps_of(arg_keys[3], (CELLS,), ((0, 32),), -0.4, 0.0), -1.0, 1.0)
    target_mass = jnp.clip(jax.random.uniform(arg_keys[4], (CELLS,), jnp.float32, -1.0, 1.0) * steps_of(arg_keys[4], (CELLS,), ((0, 32),), -0.4, 0.0), -1.0, 1.0)
    pair_list = draw_pair_list(jax.random.fold_in(arg_keys[6], 71), 0)
    return dict(source_points=source_points, target_points=target_points, target_features=target_features, source_mass=source_mass, target_mass=target_mass, pair_list=pair_list)


EPSILON = 0.1
LOWEST = -1.0e30


def merge_pair(first, second):
    higher = jnp.maximum(first[0], second[0])
    summed = first[1] * jnp.exp(first[0] - higher) + second[1] * jnp.exp(second[0] - higher)
    return higher, summed


def reference(source_points, target_points, target_features, source_mass, target_mass, pair_list):
    blocks = N_CELLS
    chosen = jnp.nonzero(pair_list[2] == 1, size=NEIGH * N_CELLS)[0].astype(jnp.int32)
    sources = pair_list[0][chosen].astype(jnp.int32)
    targets = pair_list[1][chosen].astype(jnp.int32)
    src_blocks = source_points.reshape(DIMS, blocks, BLK).transpose(1, 0, 2)
    tgt_blocks = target_points.reshape(DIMS, blocks, BLK).transpose(1, 0, 2)
    feat_blocks = target_features.reshape(blocks, BLK, FEAT)
    src_square = jnp.sum(jnp.square(src_blocks.astype(jnp.float32)), axis=1)
    tgt_square = jnp.sum(jnp.square(tgt_blocks.astype(jnp.float32)), axis=1)
    src_mass = source_mass.reshape(blocks, BLK)
    tgt_mass = target_mass.reshape(blocks, BLK)

    def cost_of(src_block, tgt_block):
        inner_products = jnp.dot(src_blocks[src_block].T, tgt_blocks[tgt_block], preferred_element_type=jnp.float32)
        return (src_square[src_block][:, None] + tgt_square[tgt_block][None, :] - 2.0 * inner_products) / DIMS

    def initial_pair():
        return (jnp.full((blocks, BLK), LOWEST, jnp.float32), jnp.zeros((blocks, BLK), jnp.float32))

    def column_pass(source_pot):
        def visit(carry, pair_entry):
            maxima, totals = carry
            src_block, tgt_block = pair_entry
            scores = (source_pot[src_block][:, None] - cost_of(src_block, tgt_block)) / EPSILON
            higher = jnp.max(scores, axis=0)
            summed = jnp.sum(jnp.exp(scores - higher[None, :]), axis=0)
            new_max, new_total = merge_pair((maxima[tgt_block], totals[tgt_block]), (higher, summed))
            return (maxima.at[tgt_block].set(new_max), totals.at[tgt_block].set(new_total)), None
        result, unused = lax.scan(visit, initial_pair(), (sources, targets))
        return result

    def row_pass(target_pot):
        def visit(carry, pair_entry):
            maxima, totals = carry
            src_block, tgt_block = pair_entry
            scores = (target_pot[tgt_block][None, :] - cost_of(src_block, tgt_block)) / EPSILON
            higher = jnp.max(scores, axis=1)
            summed = jnp.sum(jnp.exp(scores - higher[:, None]), axis=1)
            new_max, new_total = merge_pair((maxima[src_block], totals[src_block]), (higher, summed))
            return (maxima.at[src_block].set(new_max), totals.at[src_block].set(new_total)), None
        result, unused = lax.scan(visit, initial_pair(), (sources, targets))
        return result

    source_pot = jnp.zeros((blocks, BLK), jnp.float32)
    target_pot = jnp.zeros((blocks, BLK), jnp.float32)
    for iteration in range(ITERS):
        maxima, totals = column_pass(source_pot)
        target_pot = EPSILON * tgt_mass - EPSILON * (maxima + jnp.log(totals))
        maxima, totals = row_pass(target_pot)
        source_pot = EPSILON * src_mass - EPSILON * (maxima + jnp.log(totals))

    def push(accumulated, pair_entry):
        src_block, tgt_block = pair_entry
        scores = (source_pot[src_block][:, None] + target_pot[tgt_block][None, :] - cost_of(src_block, tgt_block)) / EPSILON - src_mass[src_block][:, None]
        weight = jnp.exp(scores).astype(jnp.bfloat16)
        contribution = jnp.dot(weight, feat_blocks[tgt_block], preferred_element_type=jnp.float32)
        return accumulated.at[src_block].add(contribution), None

    mapped, unused = lax.scan(push, jnp.zeros((blocks, BLK, FEAT), jnp.float32), (sources, targets))
    return source_pot.reshape(-1), target_pot.reshape(-1), mapped.reshape(blocks * BLK, FEAT).astype(jnp.bfloat16)
```

```python
import functools
import math

import jax
import jax.numpy as jnp
from jax import lax
from jax.experimental import pallas as pl
from jax.experimental.pallas import tpu as pltpu
from jax.sharding import PartitionSpec as P

REACH = 4
GROUP = 4
EPSILON = 0.1
LOWEST = -1e30
LOG2E = math.log2(math.e)
MESH = pl.DeviceIdType.MESH

PART = 64
DEPTH = 4 * PART
EXTRA = 3 * PART

WINDOW = 2 * REACH + 1
OFFSETS = [o for k in range(1, REACH + 1) for o in (k, -k)]
LIST_REACH = REACH + GROUP - 1
LIST_OFFSETS = [o for k in range(1, LIST_REACH + 1) for o in (k, -k)]


def split3(value):
    high = value.astype(jnp.bfloat16).astype(jnp.float32)
    rest = value - high
    middle = rest.astype(jnp.bfloat16).astype(jnp.float32)
    return high, middle, rest - middle


def extra_rows(first, second, cells):
    row = lax.broadcasted_iota(jnp.int32, (16, cells), 0)
    result = jnp.zeros((16, cells), jnp.float32)
    for at, part in enumerate(tuple(first) + tuple(second)):
        result = jnp.where(row == at, part, result)
    return result.astype(jnp.bfloat16)


def kernel(
    n, code_ref, x_ref, y_ref, feat_ref, smass_ref, tmass_ref,
    f_ref, g_ref, out_ref,
    lists, xw, yw, fw, xa, ya, ycol, padded, acc, aw, b1w, b2w,
    list_s, list_r, x_s, x_r, y_s, y_r, f_s, f_r, a_s, a_r, b1_s, b1_r, b2_s, b2_r, own_sem,
):
    dims, cells = x_ref.shape
    me = lax.axis_index("cells")
    scale = LOG2E / EPSILON
    factor = 2.0 * scale / dims

    def device(offset):
        return lax.rem(me + (offset + n), n)

    def copy(source, window, middle, offset, send, recv):
        return pltpu.make_async_remote_copy(
            src_ref=source,
            dst_ref=window.at[middle - offset],
            send_sem=send.at[middle - offset],
            recv_sem=recv.at[middle - offset],
            device_id=(device(offset),),
            device_id_type=MESH,
        )

    def send_all(source, window, send, recv, middle=REACH, offsets=OFFSETS):
        for offset in offsets:
            copy(source, window, middle, offset, send, recv).start()

    def arrived(source, window, send, recv, offset, middle=REACH):
        copy(source, window, middle, -offset, send, recv).wait_recv()

    def sent_all(source, window, send, recv, middle=REACH, offsets=OFFSETS):
        for offset in offsets:
            copy(source, window, middle, offset, send, recv).wait_send()

    barrier = pltpu.get_barrier_semaphore()
    for offset in LIST_OFFSETS:
        pl.semaphore_signal(barrier, inc=1, device_id=(device(offset),), device_id_type=MESH)

    padded[...] = jnp.zeros_like(padded)
    padded[0:dims, :] = x_ref[...].astype(jnp.float32)
    xw[REACH] = padded[...].astype(jnp.bfloat16)
    padded[0:dims, :] = y_ref[...].astype(jnp.float32)
    yw[REACH] = padded[...].astype(jnp.bfloat16)
    lists[LIST_REACH] = code_ref[...]

    pl.semaphore_wait(barrier, len(LIST_OFFSETS))
    send_all(lists.at[LIST_REACH], lists, list_s, list_r, LIST_REACH, LIST_OFFSETS)
    send_all(xw.at[REACH], xw, x_s, x_r)
    send_all(yw.at[REACH], yw, y_s, y_r)
    send_all(feat_ref, fw, f_s, f_r)
    own = pltpu.make_async_copy(feat_ref, fw.at[REACH], own_sem.at[0])
    own.start()

    one = jnp.ones((1, cells), jnp.float32)
    none = jnp.zeros((1, cells), jnp.float32)
    ones, nones = (one, one, one), (none, none, none)

    def squares(points):
        wide = points.astype(jnp.float32)
        return jnp.sum(wide * wide, axis=0, keepdims=True)

    def fill_source(w):
        wide = xw[w].astype(jnp.float32)
        for at, part in enumerate(split3(wide * factor)):
            xa[w, at * PART : (at + 1) * PART, :] = part.astype(jnp.bfloat16)
        xa[w, EXTRA:DEPTH, :] = jnp.zeros((PART, cells), jnp.bfloat16)

    def fill_target(ref, w):
        points = yw[w]
        for at in range(3):
            ref[at * PART : (at + 1) * PART, :] = points
        ref[EXTRA:DEPTH, :] = jnp.zeros((PART, cells), jnp.bfloat16)

    fill_source(REACH)
    fill_target(ya.at[REACH], REACH)
    fill_target(ycol, REACH)
    ycol[EXTRA : EXTRA + 16, :] = extra_rows(nones, ones, cells)

    for offset in LIST_OFFSETS:
        arrived(lists.at[LIST_REACH], lists, list_s, list_r, offset, LIST_REACH)
    codes = lists[...]

    def bias(source, target):
        hits = jnp.sum(jnp.where(codes == source * n + target, 1.0, 0.0), axis=0)
        return jnp.where(jnp.max(hits, axis=1, keepdims=True) > 0.5, 0.0, LOWEST)

    column_bias = [bias(device(w - REACH), me) for w in range(WINDOW)]
    row_bias = [bias(me, device(w - REACH)) for w in range(WINDOW)]

    for offset in OFFSETS:
        arrived(xw.at[REACH], xw, x_s, x_r, offset)
        fill_source(REACH + offset)
    for w in range(WINDOW):
        start = squares(xw[w]) * (-scale / dims) + column_bias[w]
        xa[w, EXTRA : EXTRA + 16, :] = extra_rows(ones, split3(start), cells)

    height = 256
    across = cells // height

    def reduced(lhs_ref, rhs_ref):
        def step(s, carry):
            highest, total = carry
            w, c = s // across, lax.rem(s, across)
            lhs = lhs_ref[w, :, pl.ds(pl.multiple_of(c * height, height), height)]
            scores = lax.dot_general(
                lhs, rhs_ref[...], (((0,), (0,)), ((), ())), preferred_element_type=jnp.float32
            ).reshape(height // 8, 8, cells)
            higher = jnp.maximum(highest, jnp.max(scores, axis=0))
            terms = jnp.sum(jnp.exp2(scores - higher[None]), axis=0)
            return higher, total * jnp.exp2(highest - higher) + terms

        highest, total = lax.fori_loop(
            0,
            WINDOW * across,
            step,
            (jnp.full((8, cells), LOWEST, jnp.float32), jnp.zeros((8, cells), jnp.float32)),
        )
        higher = jnp.max(highest, axis=0, keepdims=True)
        summed = jnp.sum(total * jnp.exp2(highest - higher), axis=0, keepdims=True)
        return higher + jnp.log(summed) * LOG2E

    b1w[REACH] = tmass_ref[...] * LOG2E - reduced(xa, ycol)
    send_all(b1w.at[REACH], b1w, b1_s, b1_r)
    for offset in OFFSETS:
        arrived(yw.at[REACH], yw, y_s, y_r, offset)
        fill_target(ya.at[REACH + offset], REACH + offset)
    for offset in [0] + OFFSETS:
        w = REACH + offset
        if offset != 0:
            arrived(b1w.at[REACH], b1w, b1_s, b1_r, offset)
        ya[w, EXTRA : EXTRA + 16, :] = extra_rows(split3(b1w[w] + row_bias[w]), nones, cells)

    aw[REACH] = smass_ref[...] * LOG2E - reduced(ya, xa.at[REACH])
    send_all(aw.at[REACH], aw, a_s, a_r)
    for offset in [0] + OFFSETS:
        w = REACH + offset
        if offset != 0:
            arrived(aw.at[REACH], aw, a_s, a_r, offset)
        xa[w, EXTRA : EXTRA + 16, :] = extra_rows(ones, split3(aw[w] + column_bias[w]), cells)

    b2w[REACH] = tmass_ref[...] * LOG2E - reduced(xa, ycol)
    send_all(b2w.at[REACH], b2w, b2_s, b2_r)
    g_ref[...] = b2w[REACH] * (1.0 / scale) + squares(yw[REACH]) * (1.0 / dims)
    for offset in [0] + OFFSETS:
        w = REACH + offset
        if offset != 0:
            arrived(b2w.at[REACH], b2w, b2_s, b2_r, offset)
        ya[w, EXTRA : EXTRA + 16, :] = extra_rows(split3(b2w[w] + row_bias[w]), nones, cells)

    own.wait()
    for offset in OFFSETS:
        arrived(feat_ref, fw, f_s, f_r, offset)
    acc[...] = jnp.zeros_like(acc)
    tall = 512
    pieces = cells // tall

    def mapping(s, carry):
        highest, total = carry
        w, c = s // pieces, lax.rem(s, pieces)
        start = pl.multiple_of(c * tall, tall)
        scores = lax.dot_general(
            ya[w, :, pl.ds(start, tall)], xa[REACH], (((0,), (0,)), ((), ())),
            preferred_element_type=jnp.float32,
        )
        higher = jnp.maximum(highest, jnp.max(scores, axis=0, keepdims=True))
        weight = jnp.exp2(scores - higher)
        shrink = jnp.exp2(highest - higher)
        terms = jnp.sum(weight.reshape(tall // 8, 8, cells), axis=0)
        acc[...] = acc[...] * shrink + lax.dot_general(
            fw[w, pl.ds(start, tall), :], weight.astype(jnp.bfloat16), (((0,), (0,)), ((), ())),
            preferred_element_type=jnp.float32,
        )
        return higher, total * shrink + terms

    highest, total = lax.fori_loop(
        0,
        WINDOW * pieces,
        mapping,
        (jnp.full((1, cells), LOWEST, jnp.float32), jnp.zeros((8, cells), jnp.float32)),
    )
    total = jnp.sum(total, axis=0, keepdims=True)
    last = smass_ref[...] * LOG2E - (highest + jnp.log(total) * LOG2E)
    f_ref[...] = last * (1.0 / scale) + squares(xw[REACH]) * (1.0 / dims)
    out_ref[...] = jnp.transpose(acc[...] * (1.0 / total)).astype(out_ref.dtype)

    sent_all(lists.at[LIST_REACH], lists, list_s, list_r, LIST_REACH, LIST_OFFSETS)
    sent_all(xw.at[REACH], xw, x_s, x_r)
    sent_all(yw.at[REACH], yw, y_s, y_r)
    sent_all(feat_ref, fw, f_s, f_r)
    sent_all(b1w.at[REACH], b1w, b1_s, b1_r)
    sent_all(aw.at[REACH], aw, a_s, a_r)
    sent_all(b2w.at[REACH], b2w, b2_s, b2_r)


def local(n, source_points, target_points, target_features, source_mass, target_mass, pair_list):
    cells = source_points.shape[1]
    width = target_features.shape[1]
    code = jnp.where(pair_list[2] == 1, pair_list[0] * n + pair_list[1], -1)
    code = jnp.pad(code[None, :], ((0, 0), (0, 128 - code.shape[0])), constant_values=-1)
    lists = 2 * LIST_REACH + 1
    vmem = pl.BlockSpec(memory_space=pltpu.VMEM)
    dma = pltpu.SemaphoreType.DMA
    potential, target, mapped = pl.pallas_call(
        functools.partial(kernel, n),
        out_shape=(
            jax.ShapeDtypeStruct((1, cells), jnp.float32),
            jax.ShapeDtypeStruct((1, cells), jnp.float32),
            jax.ShapeDtypeStruct((cells, width), jnp.bfloat16),
        ),
        in_specs=[vmem, vmem, vmem, pl.BlockSpec(memory_space=pl.ANY), vmem, vmem],
        out_specs=(vmem, vmem, vmem),
        scratch_shapes=[
            pltpu.VMEM((lists, 1, 128), jnp.int32),
            pltpu.VMEM((WINDOW, PART, cells), jnp.bfloat16),
            pltpu.VMEM((WINDOW, PART, cells), jnp.bfloat16),
            pltpu.VMEM((WINDOW, cells, width), jnp.bfloat16),
            pltpu.VMEM((WINDOW, DEPTH, cells), jnp.bfloat16),
            pltpu.VMEM((WINDOW, DEPTH, cells), jnp.bfloat16),
            pltpu.VMEM((DEPTH, cells), jnp.bfloat16),
            pltpu.VMEM((PART, cells), jnp.float32),
            pltpu.VMEM((width, cells), jnp.float32),
            pltpu.VMEM((WINDOW, 1, cells), jnp.float32),
            pltpu.VMEM((WINDOW, 1, cells), jnp.float32),
            pltpu.VMEM((WINDOW, 1, cells), jnp.float32),
            dma((lists,)), dma((lists,)),
        ]
        + [dma((WINDOW,))] * 12
        + [dma((1,))],
        compiler_params=pltpu.CompilerParams(
            collective_id=0, has_side_effects=True, vmem_limit_bytes=52 * 1024 * 1024
        ),
    )(
        code, source_points, target_points, target_features,
        source_mass.reshape(1, cells), target_mass.reshape(1, cells),
    )
    return potential.reshape(cells), target.reshape(cells), mapped


def solution(mesh):
    return jax.shard_map(
        functools.partial(local, mesh.shape["cells"]),
        mesh=mesh,
        in_specs=(
            P(None, "cells"),
            P(None, "cells"),
            P("cells", None),
            P("cells"),
            P("cells"),
            P(None, "cells"),
        ),
        out_specs=(P("cells"), P("cells"), P("cells", None)),
        check_vma=False,
    )
```

```python
import functools
import math

import jax
import jax.numpy as jnp
from jax import lax
from jax.experimental import pallas as pl
from jax.experimental.pallas import tpu as pltpu
from jax.sharding import PartitionSpec as P

REACH = 4
GROUP = 4
EPSILON = 0.1
LOWEST = -1e30
LOG2E = math.log2(math.e)
MESH = pl.DeviceIdType.MESH

PART = 64
DEPTH = 4 * PART
EXTRA = 3 * PART

WINDOW = 2 * REACH + 1
OFFSETS = [o for k in range(1, REACH + 1) for o in (k, -k)]
EVEN = [o for o in OFFSETS if o % 2 == 0]
RELAYED = [w for w in range(WINDOW) if (w - REACH) % 2 != 0]
LIST_REACH = REACH + GROUP - 1
LIST_OFFSETS = [o for k in range(1, LIST_REACH + 1) for o in (k, -k)]


def split3(value):
    high = value.astype(jnp.bfloat16).astype(jnp.float32)
    rest = value - high
    middle = rest.astype(jnp.bfloat16).astype(jnp.float32)
    return high, middle, rest - middle


def extra_rows(first, second, cells):
    row = lax.broadcasted_iota(jnp.int32, (16, cells), 0)
    result = jnp.zeros((16, cells), jnp.float32)
    for at, part in enumerate(tuple(first) + tuple(second)):
        result = jnp.where(row == at, part, result)
    return result.astype(jnp.bfloat16)


def kernel(
    n, code_ref, x_ref, y_ref, feat_ref, smass_ref, tmass_ref,
    f_ref, g_ref, out_ref,
    lists, xw, yw, fw, xa, ya, ycol, padded, acc, aw, b1w, b2w,
    list_s, list_r, x_s, x_r, y_s, y_r, f_s, f_r, a_s, a_r, b1_s, b1_r, b2_s, b2_r, own_sem,
):
    dims, cells = x_ref.shape
    me = lax.axis_index("cells")
    scale = LOG2E / EPSILON
    factor = 2.0 * scale / dims

    def device(offset):
        return lax.rem(me + (offset + n), n)

    def copy(source, window, middle, offset, send, recv):
        return pltpu.make_async_remote_copy(
            src_ref=source,
            dst_ref=window.at[middle - offset],
            send_sem=send.at[middle - offset],
            recv_sem=recv.at[middle - offset],
            device_id=(device(offset),),
            device_id_type=MESH,
        )

    def send_all(source, window, send, recv, middle=REACH, offsets=OFFSETS):
        for offset in offsets:
            copy(source, window, middle, offset, send, recv).start()

    def arrived(source, window, send, recv, offset, middle=REACH):
        copy(source, window, middle, -offset, send, recv).wait_recv()

    def sent_all(source, window, send, recv, middle=REACH, offsets=OFFSETS):
        for offset in offsets:
            copy(source, window, middle, offset, send, recv).wait_send()

    core = lax.rem(me, 2)
    sibling = me + 1 - 2 * core

    def relay(window, w, send, recv):
        return pltpu.make_async_remote_copy(
            src_ref=window.at[w + 1 - 2 * core],
            dst_ref=window.at[w],
            send_sem=send.at[w],
            recv_sem=recv.at[w],
            device_id=(sibling,),
            device_id_type=MESH,
        )

    def forward(source, window, send, recv):
        for offset in EVEN:
            arrived(source, window, send, recv, offset)
        for w in RELAYED:
            relay(window, w, send, recv).start()

    def relays_arrived(window, send, recv):
        for w in RELAYED:
            relay(window, w, send, recv).wait_recv()

    def relays_sent(window, send, recv):
        for w in RELAYED:
            relay(window, w, send, recv).wait_send()

    barrier = pltpu.get_barrier_semaphore()
    for offset in LIST_OFFSETS:
        pl.semaphore_signal(barrier, inc=1, device_id=(device(offset),), device_id_type=MESH)

    padded[...] = jnp.zeros_like(padded)
    padded[0:dims, :] = x_ref[...].astype(jnp.float32)
    xw[REACH] = padded[...].astype(jnp.bfloat16)
    padded[0:dims, :] = y_ref[...].astype(jnp.float32)
    yw[REACH] = padded[...].astype(jnp.bfloat16)
    lists[LIST_REACH] = code_ref[...]

    pl.semaphore_wait(barrier, len(LIST_OFFSETS))
    send_all(lists.at[LIST_REACH], lists, list_s, list_r, LIST_REACH, LIST_OFFSETS)
    send_all(xw.at[REACH], xw, x_s, x_r, offsets=EVEN)
    send_all(yw.at[REACH], yw, y_s, y_r, offsets=EVEN)
    own = pltpu.make_async_copy(feat_ref, fw.at[REACH], own_sem.at[0])
    own.start()

    one = jnp.ones((1, cells), jnp.float32)
    none = jnp.zeros((1, cells), jnp.float32)
    ones, nones = (one, one, one), (none, none, none)

    def squares(points):
        wide = points.astype(jnp.float32)
        return jnp.sum(wide * wide, axis=0, keepdims=True)

    def fill_source(w):
        wide = xw[w].astype(jnp.float32)
        for at, part in enumerate(split3(wide * factor)):
            xa[w, at * PART : (at + 1) * PART, :] = part.astype(jnp.bfloat16)
        xa[w, EXTRA:DEPTH, :] = jnp.zeros((PART, cells), jnp.bfloat16)

    def fill_target(ref, w):
        points = yw[w]
        for at in range(3):
            ref[at * PART : (at + 1) * PART, :] = points
        ref[EXTRA:DEPTH, :] = jnp.zeros((PART, cells), jnp.bfloat16)

    fill_source(REACH)
    fill_target(ya.at[REACH], REACH)
    fill_target(ycol, REACH)
    ycol[EXTRA : EXTRA + 16, :] = extra_rows(nones, ones, cells)

    for offset in LIST_OFFSETS:
        arrived(lists.at[LIST_REACH], lists, list_s, list_r, offset, LIST_REACH)
    codes = lists[...]

    def bias(source, target):
        hits = jnp.sum(jnp.where(codes == source * n + target, 1.0, 0.0), axis=0)
        return jnp.where(jnp.max(hits, axis=1, keepdims=True) > 0.5, 0.0, LOWEST)

    column_bias = [bias(device(w - REACH), me) for w in range(WINDOW)]
    row_bias = [bias(me, device(w - REACH)) for w in range(WINDOW)]

    forward(xw.at[REACH], xw, x_s, x_r)
    for offset in EVEN:
        fill_source(REACH + offset)
    relays_arrived(xw, x_s, x_r)
    for w in RELAYED:
        fill_source(w)
    for w in range(WINDOW):
        start = squares(xw[w]) * (-scale / dims) + column_bias[w]
        xa[w, EXTRA : EXTRA + 16, :] = extra_rows(ones, split3(start), cells)

    height = 256
    across = cells // height

    def reduced(lhs_ref, rhs_ref):
        def step(s, carry):
            highest, total = carry
            w, c = s // across, lax.rem(s, across)
            lhs = lhs_ref[w, :, pl.ds(pl.multiple_of(c * height, height), height)]
            scores = lax.dot_general(
                lhs, rhs_ref[...], (((0,), (0,)), ((), ())), preferred_element_type=jnp.float32
            ).reshape(height // 8, 8, cells)
            higher = jnp.maximum(highest, jnp.max(scores, axis=0))
            terms = jnp.sum(jnp.exp2(scores - higher[None]), axis=0)
            return higher, total * jnp.exp2(highest - higher) + terms

        highest, total = lax.fori_loop(
            0,
            WINDOW * across,
            step,
            (jnp.full((8, cells), LOWEST, jnp.float32), jnp.zeros((8, cells), jnp.float32)),
            unroll=2,
        )
        higher = jnp.max(highest, axis=0, keepdims=True)
        summed = jnp.sum(total * jnp.exp2(highest - higher), axis=0, keepdims=True)
        return higher + jnp.log(summed) * LOG2E

    b1w[REACH] = tmass_ref[...] * LOG2E - reduced(xa, ycol)
    send_all(b1w.at[REACH], b1w, b1_s, b1_r)
    forward(yw.at[REACH], yw, y_s, y_r)
    for offset in EVEN:
        fill_target(ya.at[REACH + offset], REACH + offset)
    relays_arrived(yw, y_s, y_r)
    for w in RELAYED:
        fill_target(ya.at[w], w)
    for offset in [0] + OFFSETS:
        w = REACH + offset
        if offset != 0:
            arrived(b1w.at[REACH], b1w, b1_s, b1_r, offset)
        ya[w, EXTRA : EXTRA + 16, :] = extra_rows(split3(b1w[w] + row_bias[w]), nones, cells)

    send_all(feat_ref, fw, f_s, f_r, offsets=EVEN)
    aw[REACH] = smass_ref[...] * LOG2E - reduced(ya, xa.at[REACH])
    send_all(aw.at[REACH], aw, a_s, a_r)
    for offset in [0] + OFFSETS:
        w = REACH + offset
        if offset != 0:
            arrived(aw.at[REACH], aw, a_s, a_r, offset)
        xa[w, EXTRA : EXTRA + 16, :] = extra_rows(ones, split3(aw[w] + column_bias[w]), cells)

    b2w[REACH] = tmass_ref[...] * LOG2E - reduced(xa, ycol)
    send_all(b2w.at[REACH], b2w, b2_s, b2_r)
    own.wait()
    forward(feat_ref, fw, f_s, f_r)
    g_ref[...] = b2w[REACH] * (1.0 / scale) + squares(yw[REACH]) * (1.0 / dims)
    for offset in [0] + OFFSETS:
        w = REACH + offset
        if offset != 0:
            arrived(b2w.at[REACH], b2w, b2_s, b2_r, offset)
        ya[w, EXTRA : EXTRA + 16, :] = extra_rows(split3(b2w[w] + row_bias[w]), nones, cells)

    relays_arrived(fw, f_s, f_r)
    acc[...] = jnp.zeros_like(acc)
    tall = 512
    pieces = cells // tall

    def mapping(s, carry):
        highest, total = carry
        w, c = s // pieces, lax.rem(s, pieces)
        start = pl.multiple_of(c * tall, tall)
        scores = lax.dot_general(
            ya[w, :, pl.ds(start, tall)], xa[REACH], (((0,), (0,)), ((), ())),
            preferred_element_type=jnp.float32,
        )
        higher = jnp.maximum(highest, jnp.max(scores, axis=0, keepdims=True))
        weight = jnp.exp2(scores - higher)
        shrink = jnp.exp2(highest - higher)
        terms = jnp.sum(weight.reshape(tall // 8, 8, cells), axis=0)
        acc[...] = acc[...] * shrink + lax.dot_general(
            fw[w, pl.ds(start, tall), :], weight.astype(jnp.bfloat16), (((0,), (0,)), ((), ())),
            preferred_element_type=jnp.float32,
        )
        return higher, total * shrink + terms

    highest, total = lax.fori_loop(
        0,
        WINDOW * pieces,
        mapping,
        (jnp.full((1, cells), LOWEST, jnp.float32), jnp.zeros((8, cells), jnp.float32)),
    )
    total = jnp.sum(total, axis=0, keepdims=True)
    last = smass_ref[...] * LOG2E - (highest + jnp.log(total) * LOG2E)
    f_ref[...] = last * (1.0 / scale) + squares(xw[REACH]) * (1.0 / dims)
    out_ref[...] = jnp.transpose(acc[...] * (1.0 / total)).astype(out_ref.dtype)

    sent_all(lists.at[LIST_REACH], lists, list_s, list_r, LIST_REACH, LIST_OFFSETS)
    sent_all(xw.at[REACH], xw, x_s, x_r, offsets=EVEN)
    sent_all(yw.at[REACH], yw, y_s, y_r, offsets=EVEN)
    sent_all(feat_ref, fw, f_s, f_r, offsets=EVEN)
    relays_sent(xw, x_s, x_r)
    relays_sent(yw, y_s, y_r)
    relays_sent(fw, f_s, f_r)
    sent_all(b1w.at[REACH], b1w, b1_s, b1_r)
    sent_all(aw.at[REACH], aw, a_s, a_r)
    sent_all(b2w.at[REACH], b2w, b2_s, b2_r)


def local(n, source_points, target_points, target_features, source_mass, target_mass, pair_list):
    cells = source_points.shape[1]
    width = target_features.shape[1]
    code = jnp.where(pair_list[2] == 1, pair_list[0] * n + pair_list[1], -1)
    code = jnp.pad(code[None, :], ((0, 0), (0, 128 - code.shape[0])), constant_values=-1)
    lists = 2 * LIST_REACH + 1
    vmem = pl.BlockSpec(memory_space=pltpu.VMEM)
    dma = pltpu.SemaphoreType.DMA
    potential, target, mapped = pl.pallas_call(
        functools.partial(kernel, n),
        out_shape=(
            jax.ShapeDtypeStruct((1, cells), jnp.float32),
            jax.ShapeDtypeStruct((1, cells), jnp.float32),
            jax.ShapeDtypeStruct((cells, width), jnp.bfloat16),
        ),
        in_specs=[vmem, vmem, vmem, pl.BlockSpec(memory_space=pl.ANY), vmem, vmem],
        out_specs=(vmem, vmem, vmem),
        scratch_shapes=[
            pltpu.VMEM((lists, 1, 128), jnp.int32),
            pltpu.VMEM((WINDOW, PART, cells), jnp.bfloat16),
            pltpu.VMEM((WINDOW, PART, cells), jnp.bfloat16),
            pltpu.VMEM((WINDOW, cells, width), jnp.bfloat16),
            pltpu.VMEM((WINDOW, DEPTH, cells), jnp.bfloat16),
            pltpu.VMEM((WINDOW, DEPTH, cells), jnp.bfloat16),
            pltpu.VMEM((DEPTH, cells), jnp.bfloat16),
            pltpu.VMEM((PART, cells), jnp.float32),
            pltpu.VMEM((width, cells), jnp.float32),
            pltpu.VMEM((WINDOW, 1, cells), jnp.float32),
            pltpu.VMEM((WINDOW, 1, cells), jnp.float32),
            pltpu.VMEM((WINDOW, 1, cells), jnp.float32),
            dma((lists,)), dma((lists,)),
        ]
        + [dma((WINDOW,))] * 12
        + [dma((1,))],
        compiler_params=pltpu.CompilerParams(
            collective_id=0, has_side_effects=True, vmem_limit_bytes=52 * 1024 * 1024
        ),
    )(
        code, source_points, target_points, target_features,
        source_mass.reshape(1, cells), target_mass.reshape(1, cells),
    )
    return potential.reshape(cells), target.reshape(cells), mapped


def solution(mesh):
    return jax.shard_map(
        functools.partial(local, mesh.shape["cells"]),
        mesh=mesh,
        in_specs=(
            P(None, "cells"),
            P(None, "cells"),
            P("cells", None),
            P("cells"),
            P("cells"),
            P(None, "cells"),
        ),
        out_specs=(P("cells"), P("cells"), P("cells", None)),
        check_vma=False,
    )
```

```python
import functools
import math

import jax
import jax.numpy as jnp
from jax import lax
from jax.experimental import pallas as pl
from jax.experimental.pallas import tpu as pltpu
from jax.sharding import PartitionSpec as P

REACH = 4
GROUP = 4
NEIGH = 7
EPSILON = 0.1
LOWEST = -1e30
LOG2E = math.log2(math.e)
MESH = pl.DeviceIdType.MESH

PART = 64
DEPTH = 4 * PART
EXTRA = 3 * PART

WINDOW = 2 * REACH + 1
OFFSETS = [o for k in range(1, REACH + 1) for o in (k, -k)]
EVEN = [o for o in OFFSETS if o % 2 == 0]
RELAYED = [w for w in range(WINDOW) if (w - REACH) % 2 != 0]
LIST_REACH = REACH + GROUP - 1
LIST_OFFSETS = [o for k in range(1, LIST_REACH + 1) for o in (k, -k)]


def split3(value):
    high = value.astype(jnp.bfloat16).astype(jnp.float32)
    rest = value - high
    middle = rest.astype(jnp.bfloat16).astype(jnp.float32)
    return high, middle, rest - middle


def extra_rows(first, second, cells):
    row = lax.broadcasted_iota(jnp.int32, (16, cells), 0)
    result = jnp.zeros((16, cells), jnp.float32)
    for at, part in enumerate(tuple(first) + tuple(second)):
        result = jnp.where(row == at, part, result)
    return result.astype(jnp.bfloat16)


def kernel(
    n, code_ref, x_ref, y_ref, feat_ref, smass_ref, tmass_ref,
    f_ref, g_ref, out_ref,
    paired, lists, xw, yw, fw, xa, ya, ycol, padded, acc, aw, b1w, b2w,
    list_s, list_r, x_s, x_r, y_s, y_r, f_s, f_r, a_s, a_r, b1_s, b1_r, b2_s, b2_r, own_sem,
):
    dims, cells = x_ref.shape
    me = lax.axis_index("cells")
    scale = LOG2E / EPSILON
    factor = 2.0 * scale / dims

    def device(offset):
        return lax.rem(me + (offset + n), n)

    def copy(source, window, middle, offset, send, recv):
        return pltpu.make_async_remote_copy(
            src_ref=source,
            dst_ref=window.at[middle - offset],
            send_sem=send.at[middle - offset],
            recv_sem=recv.at[middle - offset],
            device_id=(device(offset),),
            device_id_type=MESH,
        )

    def send_all(source, window, send, recv, middle=REACH, offsets=OFFSETS):
        for offset in offsets:
            copy(source, window, middle, offset, send, recv).start()

    def arrived(source, window, send, recv, offset, middle=REACH):
        copy(source, window, middle, -offset, send, recv).wait_recv()

    def sent_all(source, window, send, recv, middle=REACH, offsets=OFFSETS):
        for offset in offsets:
            copy(source, window, middle, offset, send, recv).wait_send()

    core = lax.rem(me, 2)
    sibling = me + 1 - 2 * core

    def relay(window, w, send, recv):
        return pltpu.make_async_remote_copy(
            src_ref=window.at[w + 1 - 2 * core],
            dst_ref=window.at[w],
            send_sem=send.at[w],
            recv_sem=recv.at[w],
            device_id=(sibling,),
            device_id_type=MESH,
        )

    def forward(source, window, send, recv):
        for offset in EVEN:
            arrived(source, window, send, recv, offset)
        for w in RELAYED:
            relay(window, w, send, recv).start()

    def relays_arrived(window, send, recv):
        for w in RELAYED:
            relay(window, w, send, recv).wait_recv()

    def relays_sent(window, send, recv):
        for w in RELAYED:
            relay(window, w, send, recv).wait_send()

    barrier = pltpu.get_barrier_semaphore()
    for offset in LIST_OFFSETS:
        pl.semaphore_signal(barrier, inc=1, device_id=(device(offset),), device_id_type=MESH)

    padded[...] = jnp.zeros_like(padded)
    padded[0:dims, :] = x_ref[...].astype(jnp.float32)
    xw[REACH] = padded[...].astype(jnp.bfloat16)
    padded[0:dims, :] = y_ref[...].astype(jnp.float32)
    yw[REACH] = padded[...].astype(jnp.bfloat16)
    lists[LIST_REACH] = code_ref[...]

    pl.semaphore_wait(barrier, len(LIST_OFFSETS))
    send_all(lists.at[LIST_REACH], lists, list_s, list_r, LIST_REACH, LIST_OFFSETS)
    send_all(xw.at[REACH], xw, x_s, x_r, offsets=EVEN)
    send_all(yw.at[REACH], yw, y_s, y_r, offsets=EVEN)
    own = pltpu.make_async_copy(feat_ref, fw.at[REACH], own_sem.at[0])
    own.start()

    one = jnp.ones((1, cells), jnp.float32)
    none = jnp.zeros((1, cells), jnp.float32)
    ones, nones = (one, one, one), (none, none, none)

    def squares(points):
        wide = points.astype(jnp.float32)
        return jnp.sum(wide * wide, axis=0, keepdims=True)

    def fill_source(w):
        wide = xw[w].astype(jnp.float32)
        for at, part in enumerate(split3(wide * factor)):
            xa[w, at * PART : (at + 1) * PART, :] = part.astype(jnp.bfloat16)
        xa[w, EXTRA:DEPTH, :] = jnp.zeros((PART, cells), jnp.bfloat16)

    def fill_target(ref, w):
        points = yw[w]
        for at in range(3):
            ref[at * PART : (at + 1) * PART, :] = points
        ref[EXTRA:DEPTH, :] = jnp.zeros((PART, cells), jnp.bfloat16)

    fill_source(REACH)
    fill_target(ya.at[REACH], REACH)
    fill_target(ycol, REACH)
    ycol[EXTRA : EXTRA + 16, :] = extra_rows(nones, ones, cells)

    for offset in LIST_OFFSETS:
        arrived(lists.at[LIST_REACH], lists, list_s, list_r, offset, LIST_REACH)
    codes = lists[...]

    def bias(source, target):
        hits = jnp.sum(jnp.where(codes == source * n + target, 1.0, 0.0), axis=0)
        return jnp.where(jnp.max(hits, axis=1, keepdims=True) > 0.5, 0.0, LOWEST)

    column_bias = [bias(device(w - REACH), me) for w in range(WINDOW)]
    live = [
        jnp.max(jnp.where(codes == me * n + device(w - REACH), 1, 0)) for w in range(WINDOW)
    ]
    entries = [jnp.int32(REACH)] * NEIGH
    rank = jnp.int32(0)
    for w in range(WINDOW):
        for k in range(NEIGH):
            entries[k] = jnp.where((rank == k) & (live[w] == 1), w, entries[k])
        rank = rank + live[w]
    for k in range(NEIGH):
        paired[k] = entries[k]

    forward(xw.at[REACH], xw, x_s, x_r)
    for offset in EVEN:
        fill_source(REACH + offset)
    relays_arrived(xw, x_s, x_r)
    for w in RELAYED:
        fill_source(w)
    for w in range(WINDOW):
        start = squares(xw[w]) * (-scale / dims) + column_bias[w]
        xa[w, EXTRA : EXTRA + 16, :] = extra_rows(ones, split3(start), cells)

    height = 256
    across = cells // height

    def reduced(lhs_ref, rhs_ref, visits, entry):
        def step(s, carry):
            highest, total = carry
            w, c = entry(s // across), lax.rem(s, across)
            lhs = lhs_ref[w, :, pl.ds(pl.multiple_of(c * height, height), height)]
            scores = lax.dot_general(
                lhs, rhs_ref[...], (((0,), (0,)), ((), ())), preferred_element_type=jnp.float32
            ).reshape(height // 8, 8, cells)
            higher = jnp.maximum(highest, jnp.max(scores, axis=0))
            terms = jnp.sum(jnp.exp2(scores - higher[None]), axis=0)
            return higher, total * jnp.exp2(highest - higher) + terms

        highest, total = lax.fori_loop(
            0,
            visits * across,
            step,
            (jnp.full((8, cells), LOWEST, jnp.float32), jnp.zeros((8, cells), jnp.float32)),
            unroll=2,
        )
        higher = jnp.max(highest, axis=0, keepdims=True)
        summed = jnp.sum(total * jnp.exp2(highest - higher), axis=0, keepdims=True)
        return higher + jnp.log(summed) * LOG2E

    b1w[REACH] = tmass_ref[...] * LOG2E - reduced(xa, ycol, WINDOW, lambda w: w)
    send_all(b1w.at[REACH], b1w, b1_s, b1_r)
    forward(yw.at[REACH], yw, y_s, y_r)
    for offset in EVEN:
        fill_target(ya.at[REACH + offset], REACH + offset)
    relays_arrived(yw, y_s, y_r)
    for w in RELAYED:
        fill_target(ya.at[w], w)
    for offset in [0] + OFFSETS:
        w = REACH + offset
        if offset != 0:
            arrived(b1w.at[REACH], b1w, b1_s, b1_r, offset)
        ya[w, EXTRA : EXTRA + 16, :] = extra_rows(split3(b1w[w]), nones, cells)

    send_all(feat_ref, fw, f_s, f_r, offsets=EVEN)
    aw[REACH] = smass_ref[...] * LOG2E - reduced(ya, xa.at[REACH], NEIGH, lambda k: paired[k])
    send_all(aw.at[REACH], aw, a_s, a_r)
    for offset in [0] + OFFSETS:
        w = REACH + offset
        if offset != 0:
            arrived(aw.at[REACH], aw, a_s, a_r, offset)
        xa[w, EXTRA : EXTRA + 16, :] = extra_rows(ones, split3(aw[w] + column_bias[w]), cells)

    b2w[REACH] = tmass_ref[...] * LOG2E - reduced(xa, ycol, WINDOW, lambda w: w)
    send_all(b2w.at[REACH], b2w, b2_s, b2_r)
    own.wait()
    forward(feat_ref, fw, f_s, f_r)
    g_ref[...] = b2w[REACH] * (1.0 / scale) + squares(yw[REACH]) * (1.0 / dims)
    for offset in [0] + OFFSETS:
        w = REACH + offset
        if offset != 0:
            arrived(b2w.at[REACH], b2w, b2_s, b2_r, offset)
        ya[w, EXTRA : EXTRA + 16, :] = extra_rows(split3(b2w[w]), nones, cells)

    relays_arrived(fw, f_s, f_r)
    acc[...] = jnp.zeros_like(acc)
    tall = 512
    pieces = cells // tall

    def mapping(s, carry):
        highest, total = carry
        w, c = paired[s // pieces], lax.rem(s, pieces)
        start = pl.multiple_of(c * tall, tall)
        scores = lax.dot_general(
            ya[w, :, pl.ds(start, tall)], xa[REACH], (((0,), (0,)), ((), ())),
            preferred_element_type=jnp.float32,
        )
        higher = jnp.maximum(highest, jnp.max(scores, axis=0, keepdims=True))
        weight = jnp.exp2(scores - higher)
        shrink = jnp.exp2(highest - higher)
        terms = jnp.sum(weight.reshape(tall // 8, 8, cells), axis=0)
        acc[...] = acc[...] * shrink + lax.dot_general(
            fw[w, pl.ds(start, tall), :], weight.astype(jnp.bfloat16), (((0,), (0,)), ((), ())),
            preferred_element_type=jnp.float32,
        )
        return higher, total * shrink + terms

    highest, total = lax.fori_loop(
        0,
        NEIGH * pieces,
        mapping,
        (jnp.full((1, cells), LOWEST, jnp.float32), jnp.zeros((8, cells), jnp.float32)),
    )
    total = jnp.sum(total, axis=0, keepdims=True)
    last = smass_ref[...] * LOG2E - (highest + jnp.log(total) * LOG2E)
    f_ref[...] = last * (1.0 / scale) + squares(xw[REACH]) * (1.0 / dims)
    out_ref[...] = jnp.transpose(acc[...] * (1.0 / total)).astype(out_ref.dtype)

    sent_all(lists.at[LIST_REACH], lists, list_s, list_r, LIST_REACH, LIST_OFFSETS)
    sent_all(xw.at[REACH], xw, x_s, x_r, offsets=EVEN)
    sent_all(yw.at[REACH], yw, y_s, y_r, offsets=EVEN)
    sent_all(feat_ref, fw, f_s, f_r, offsets=EVEN)
    relays_sent(xw, x_s, x_r)
    relays_sent(yw, y_s, y_r)
    relays_sent(fw, f_s, f_r)
    sent_all(b1w.at[REACH], b1w, b1_s, b1_r)
    sent_all(aw.at[REACH], aw, a_s, a_r)
    sent_all(b2w.at[REACH], b2w, b2_s, b2_r)


def local(n, source_points, target_points, target_features, source_mass, target_mass, pair_list):
    cells = source_points.shape[1]
    width = target_features.shape[1]
    code = jnp.where(pair_list[2] == 1, pair_list[0] * n + pair_list[1], -1)
    code = jnp.pad(code[None, :], ((0, 0), (0, 128 - code.shape[0])), constant_values=-1)
    lists = 2 * LIST_REACH + 1
    vmem = pl.BlockSpec(memory_space=pltpu.VMEM)
    dma = pltpu.SemaphoreType.DMA
    potential, target, mapped = pl.pallas_call(
        functools.partial(kernel, n),
        out_shape=(
            jax.ShapeDtypeStruct((1, cells), jnp.float32),
            jax.ShapeDtypeStruct((1, cells), jnp.float32),
            jax.ShapeDtypeStruct((cells, width), jnp.bfloat16),
        ),
        in_specs=[vmem, vmem, vmem, pl.BlockSpec(memory_space=pl.ANY), vmem, vmem],
        out_specs=(vmem, vmem, vmem),
        scratch_shapes=[
            pltpu.SMEM((NEIGH,), jnp.int32),
            pltpu.VMEM((lists, 1, 128), jnp.int32),
            pltpu.VMEM((WINDOW, PART, cells), jnp.bfloat16),
            pltpu.VMEM((WINDOW, PART, cells), jnp.bfloat16),
            pltpu.VMEM((WINDOW, cells, width), jnp.bfloat16),
            pltpu.VMEM((WINDOW, DEPTH, cells), jnp.bfloat16),
            pltpu.VMEM((WINDOW, DEPTH, cells), jnp.bfloat16),
            pltpu.VMEM((DEPTH, cells), jnp.bfloat16),
            pltpu.VMEM((PART, cells), jnp.float32),
            pltpu.VMEM((width, cells), jnp.float32),
            pltpu.VMEM((WINDOW, 1, cells), jnp.float32),
            pltpu.VMEM((WINDOW, 1, cells), jnp.float32),
            pltpu.VMEM((WINDOW, 1, cells), jnp.float32),
            dma((lists,)), dma((lists,)),
        ]
        + [dma((WINDOW,))] * 12
        + [dma((1,))],
        compiler_params=pltpu.CompilerParams(
            collective_id=0, has_side_effects=True, vmem_limit_bytes=52 * 1024 * 1024
        ),
    )(
        code, source_points, target_points, target_features,
        source_mass.reshape(1, cells), target_mass.reshape(1, cells),
    )
    return potential.reshape(cells), target.reshape(cells), mapped


def solution(mesh):
    return jax.shard_map(
        functools.partial(local, mesh.shape["cells"]),
        mesh=mesh,
        in_specs=(
            P(None, "cells"),
            P(None, "cells"),
            P("cells", None),
            P("cells"),
            P("cells"),
            P(None, "cells"),
        ),
        out_specs=(P("cells"), P("cells"), P("cells", None)),
        check_vma=False,
    )
```
